1024 devices in a mesh: dp: 16 (over z_lo, core), fsdp: 64 (over z_hi, y, x).
Axes of the slice: x: 4, y: 8, z: 16 (z_hi: 2, z_lo: 8; z = z_hi * 8 + z_lo), core: 2. Of those that a mesh axis runs over, the one named last changes fastest.
Arguments:
- gradients: bfloat16 [16, 24576, 2048], P('dp', 'fsdp'), may hold values from -6 to 6
- master: float32 [24576, 2048], P('fsdp', 'dp'), may hold values from -1.3 to 1.3
- moment_one: float32 [24576, 2048], P('fsdp', 'dp'), may hold values from -4 to 4
- moment_two: float32 [24576, 2048], P('fsdp', 'dp'), may hold values from 0.01 to 0.1
- synced: bfloat16 [24576, 2048], P('fsdp', 'dp'), may hold values from -0.75 to 0.75
- rollout: bfloat16 [24576, 2048], P('fsdp', 'dp'), may hold values from -0.77 to 0.77
- amax_record: float32 [192, 16], P('fsdp', 'dp'), may hold values from 0.04 to 1.5
- row_table: int32 [128], replicated, may hold values from 0 to 63, as said below
- expert_owner: int32 [4], replicated, may hold values from 0 to 63
Outputs:
- new_master: float32 [24576, 2048], P('fsdp', 'dp')
- new_one: float32 [24576, 2048], P('fsdp', 'dp')
- new_two: float32 [24576, 2048], P('fsdp', 'dp')
- new_amax: float32 [192, 16], P('fsdp', 'dp')
- new_rollout: bfloat16 [24576, 2048], P('fsdp', 'dp')
The draws below stay inside these ranges and needn't reach their ends.
Inputs may be any that keep to these rules, and one draw needn't show every extreme that they name: `row_table`: each of 0..63 appears exactly 2 times.
All inputs are finite; a program needn't handle non-finite values.
Results may differ from the reference program's by a relative error of at most 0.014.
Values may be sent and summed in bfloat16 or wider, within the bound.
No kernel may reach another device: no remote copies, remote signals or barrier semaphores. Data moves between devices by JAX's collectives and lax.ppermute only.
A program may use at most 32 MiB of HBM per device.

```python
import math
import jax
import jax.numpy as jnp
from jax import lax

D = 7168
F = 2048
TILE = 128
ROWS_OWN = 2
WROWS = 24576
EXP_WIN = 4
N_DP = 16
N_FSDP = 64


def base_weights(key):
    key = jax.random.fold_in(key, 17)
    return 0.25 * jnp.clip(jax.random.normal(key, (WROWS, F), jnp.float32), -3.0, 3.0)


def drift_scales(key):
    key = jax.random.fold_in(key, 19)
    return jnp.exp(jax.random.uniform(key, (WROWS // TILE, F // TILE), jnp.float32, math.log(0.1), math.log(0.5)))


def row_classes(key):
    key = jax.random.fold_in(key, 11)
    return (jax.random.permutation(key, TILE) // ROWS_OWN).astype(jnp.int32)


def owner_shifts(key):
    key = jax.random.fold_in(key, 13)
    key_values, key_top, key_low = jax.random.split(key, 3)
    values = jax.random.randint(key_values, (EXP_WIN,), 0, N_FSDP).astype(jnp.int32)
    positions = jnp.arange(EXP_WIN, dtype=jnp.int32)
    top_slot = jax.random.randint(key_top, (), 0, EXP_WIN).astype(jnp.int32)
    values = jnp.where(positions == top_slot, N_FSDP - 1, values)
    if EXP_WIN > 1:
        low_slot = (top_slot + 1 + jax.random.randint(key_low, (), 0, EXP_WIN - 1).astype(jnp.int32)) % EXP_WIN
        values = jnp.where(positions == low_slot, 0, values)
    return values.astype(jnp.int32)


def rollout_order(values, classes, owners):
    block_count = WROWS // TILE
    ordering = jnp.argsort(classes, stable=True).astype(jnp.int32)
    blocks = jnp.arange(block_count, dtype=jnp.int32)
    shifts = owners[blocks * TILE // D]
    first_slot = (jnp.arange(N_FSDP, dtype=jnp.int32)[None, :] - shifts[:, None]) % N_FSDP * ROWS_OWN
    chosen = ordering[first_slot[:, :, None] + jnp.arange(ROWS_OWN, dtype=jnp.int32)[None, None, :]]
    gathered = values.reshape(block_count, TILE, F)[blocks[:, None, None], chosen]
    return jnp.transpose(gathered, (1, 0, 2, 3)).reshape(WROWS, F)


def draw_row_table(key, part):
    classes = row_classes(key)
    return classes


def draw_expert_owner(key, part):
    owners = owner_shifts(key)
    return owners


def draw_master(key, part):
    weights = base_weights(key)
    amplitude = drift_scales(key)
    key = jax.random.fold_in(key, 23)
    spread = jax.random.uniform(key, (WROWS, F), jnp.float32, -1.0, 1.0)
    widened = jnp.repeat(jnp.repeat(amplitude, TILE, axis=0), TILE, axis=1)
    return weights + widened * spread


def draw_synced(key, part):
    weights = base_weights(key)
    return weights.astype(jnp.bfloat16)


def draw_rollout(key, part):
    weights = base_weights(key)
    classes = row_classes(key)
    owners = owner_shifts(key)
    key = jax.random.fold_in(key, 25)
    jitter = 0.02 * jax.random.uniform(key, (WROWS, F), jnp.float32, -1.0, 1.0)
    return (rollout_order(weights, classes, owners) + jitter).astype(jnp.bfloat16)


def draw_amax_record(key, part):
    amplitude = drift_scales(key)
    key = jax.random.fold_in(key, 26)
    factor = jnp.exp(jax.random.uniform(key, (WROWS // TILE, F // TILE), jnp.float32, math.log(0.4), math.log(3.0)))
    return amplitude * factor


def raised(result, own_key, source, target, shards_of, factor):
    def block_of(axis_at):
        return (jnp.arange(result.shape[axis_at]) // (result.shape[axis_at] // shards_of)).reshape((-1,) + (1,) * (result.ndim - 1 - axis_at))

    one_side = jax.random.permutation(own_key, shards_of)[block_of(target)]
    far = (block_of(target) + shards_of // 2) % shards_of
    return jnp.where((block_of(source) == one_side) | (block_of(source) == far), factor * result, result)


def block_levels(stream_key, shape, pieces, low, largest):
    def one(axis_at, blocks):
        draws = jax.random.uniform(jax.random.fold_in(jax.random.fold_in(stream_key, 6), axis_at), (blocks,), jnp.float32, low / len(pieces), largest / len(pieces))
        return jnp.repeat(jnp.exp(draws), shape[axis_at] // blocks).reshape((-1,) + (1,) * (len(shape) - axis_at - 1))

    factor_of = one(*pieces[0])
    for cut in pieces[1:]:
        factor_of = factor_of * one(*cut)
    return factor_of


def gaussian(key, shape, scale, reach, cuts=(), held_as=jnp.bfloat16):
    entries = scale * jax.random.normal(key, shape, jnp.float32)
    if cuts:
        entries = entries * block_levels(key, shape, cuts, -0.22, 0.18)
    return jnp.clip(entries, -reach, reach).astype(held_as)


def gaussian_with(own_key, shape, scale, bound, cuts, heavy, kind=jnp.bfloat16):
    drawn = scale * jax.random.normal(own_key, shape, jnp.float32)
    if cuts:
        drawn = drawn * block_levels(own_key, shape, cuts, -0.22, 0.18)
    return jnp.clip(raised(drawn, jax.random.fold_in(own_key, 3), *heavy), -bound, bound).astype(kind)


def setup_inputs(seed: int = 0) -> dict:
    key_of = jax.random.split(jax.random.key(seed), 10)
    return {
        "gradients": gaussian_with(key_of[0], (N_DP, WROWS, F), 1.0, 6.0, ((0, 16), (1, 64)), (0, 2, 16, 2.0)),
        "master": draw_master(jax.random.fold_in(key_of[9], 71), 0),
        "moment_one": gaussian(key_of[2], (WROWS, F), 0.3, 4.0, ((0, 64), (1, 16)), jnp.float32),
        "moment_two": jnp.clip(jnp.exp(math.log(0.1) - 2.3025851 * jax.random.uniform(key_of[3], (WROWS, F), jnp.float32) ** block_levels(key_of[3], (WROWS, F), ((0, 64), (1, 16)), -0.2, 0.2)), 0.01, 0.1),
        "synced": draw_synced(jax.random.fold_in(key_of[9], 71), 0),
        "rollout": draw_rollout(jax.random.fold_in(key_of[9], 71), 0),
        "amax_record": draw_amax_record(jax.random.fold_in(key_of[9], 71), 0),
        "row_table": draw_row_table(jax.random.fold_in(key_of[9], 71), 0),
        "expert_owner": draw_expert_owner(jax.random.fold_in(key_of[9], 71), 0),
    }


beta_one = 0.9
beta_two = 0.95
bias_one = 1.0 - 0.9 ** 10
bias_two = 1.0 - 0.95 ** 10
step_size = 0.05
weight_decay = 0.1
adam_floor = 1e-08
code_limit = 448.0

def adam_step(master, moment_one, moment_two, gradient):
    new_one = beta_one * moment_one + (1.0 - beta_one) * gradient
    new_two = beta_two * moment_two + (1.0 - beta_two) * gradient * gradient
    update = new_one / bias_one / (jnp.sqrt(new_two / bias_two) + adam_floor)
    new_master = master - step_size * (update + weight_decay * master)
    return (new_master, new_one, new_two)

def owner_rows(row_table, expert_owner, blocks, owner_count):
    per_owner = TILE // owner_count
    ordering = jnp.argsort(row_table, stable=True).astype(jnp.int32)
    experts = (blocks * TILE // D).astype(jnp.int32)
    shifts = expert_owner[experts]
    owners = jnp.arange(owner_count, dtype=jnp.int32)
    first_slot = (owners[None, :] - shifts[:, None]) % owner_count * per_owner
    return ordering[first_slot[:, :, None] + jnp.arange(per_owner, dtype=jnp.int32)[None, None, :]]

def reference(gradients, master, moment_one, moment_two, synced, rollout, amax_record, row_table, expert_owner):
    summed = jnp.zeros(master.shape, jnp.float32)
    for replica in range(N_DP):
        summed = summed + gradients[replica].astype(jnp.float32)
    new_master, new_one, new_two = adam_step(master, moment_one, moment_two, summed / N_DP)
    difference = new_master - synced.astype(jnp.float32)
    block_count = WROWS // TILE
    tile_count = F // TILE
    tiled_delta = difference.reshape(block_count, TILE, tile_count, TILE)
    new_amax = lax.optimization_barrier(jnp.max(jnp.abs(tiled_delta), axis=(1, 3)))
    scales = amax_record / code_limit
    code_values = jnp.clip(tiled_delta / scales[:, None, :, None], -code_limit, code_limit).astype(jnp.bfloat16)
    restored = (code_values.astype(jnp.float32) * scales[:, None, :, None]).reshape(block_count, TILE, F)
    chosen = owner_rows(row_table, expert_owner, jnp.arange(block_count, dtype=jnp.int32), N_FSDP)
    picked_rows = restored[jnp.arange(block_count, dtype=jnp.int32)[:, None, None], chosen]
    regrouped = jnp.transpose(picked_rows, (1, 0, 2, 3)).reshape(WROWS, F)
    new_rollout = (rollout.astype(jnp.float32) + regrouped).astype(jnp.bfloat16)
    return (new_master, new_one, new_two, new_amax, new_rollout)
```

```python
import jax
import jax.numpy as jnp
from jax import lax
from jax.sharding import PartitionSpec as P

D = 7168
TILE = 128

beta_one = 0.9
beta_two = 0.95
bias_one = 1.0 - 0.9**10
bias_two = 1.0 - 0.95**10
step_size = 0.05
weight_decay = 0.1
adam_floor = 1e-08


def adam_step(master, moment_one, moment_two, gradient):
    new_one = beta_one * moment_one + (1.0 - beta_one) * gradient
    new_two = beta_two * moment_two + (1.0 - beta_two) * gradient * gradient
    update = new_one / bias_one / (jnp.sqrt(new_two / bias_two) + adam_floor)
    new_master = master - step_size * (update + weight_decay * master)
    return (new_master, new_one, new_two)


def exchange(x, bit, replica_count):
    return lax.ppermute(x, "dp", [(i, i ^ bit) for i in range(replica_count)])


def half(x, index):
    return lax.dynamic_index_in_dim(x, index, axis=1, keepdims=False)


def wide(*terms):
    total = terms[0].astype(jnp.float32)
    for term in terms[1:]:
        total = total + term.astype(jnp.float32)
    return total


def body(
    gradients, master, moment_one, moment_two, synced, rollout, amax_record, row_table, expert_owner
):
    owner_count = lax.axis_size("fsdp")
    replica_count = lax.axis_size("dp")
    row_count, column_count = master.shape
    block_count = row_count // TILE
    per_owner = TILE // owner_count
    place = lax.axis_index("dp").astype(jnp.uint32)

    kept = gradients[0].reshape(row_count, replica_count // 2, 2, column_count).transpose(1, 2, 0, 3)
    core = place & 1
    terms = [half(kept, core)]
    received = exchange(half(kept, 1 - core), 1, replica_count)
    terms.append(received)
    bit = 2
    while bit < replica_count:
        mine = (place >> (bit.bit_length() - 1)) & 1
        pairs = [t.reshape(t.shape[0] // 2, 2, row_count, column_count) for t in terms]
        sending = wide(*[half(t, 1 - mine) for t in pairs]).astype(jnp.bfloat16)
        terms = [half(t, mine) for t in pairs]
        terms.append(exchange(sending, bit, replica_count))
        bit *= 2
    summed = wide(*[t[0] for t in terms])

    new_master, new_one, new_two = adam_step(master, moment_one, moment_two, summed / replica_count)
    difference = new_master - synced.astype(jnp.float32)
    tiled_delta = difference.reshape(block_count, TILE, TILE)
    new_amax = jnp.max(jnp.abs(tiled_delta), axis=(1, 2)).reshape(block_count, 1)
    limit = amax_record.reshape(block_count, 1, 1)
    clipped = jnp.clip(tiled_delta, -limit, limit).astype(jnp.bfloat16).reshape(row_count, column_count)

    rows = jnp.arange(TILE, dtype=jnp.int32)
    before = (row_table[None, :] < row_table[:, None]) | (
        (row_table[None, :] == row_table[:, None]) & (rows[None, :] < rows[:, None])
    )
    rank = jnp.sum(before.astype(jnp.int32), axis=1)
    blocks = jnp.arange(block_count, dtype=jnp.int32)
    experts = (lax.axis_index("fsdp") * block_count + blocks) * TILE // D
    shifts = expert_owner[experts]
    owner = (rank[None, :] // per_owner + shifts[:, None]) % owner_count
    slot = (owner * block_count + blocks[:, None]) * per_owner + rank[None, :] % per_owner
    chooser = (
        jnp.arange(row_count, dtype=jnp.int32)[:, None] == slot.reshape(1, row_count)
    ).astype(jnp.bfloat16)
    outgoing = lax.dot(chooser, clipped, preferred_element_type=jnp.float32).astype(jnp.bfloat16)
    incoming = lax.all_to_all(
        outgoing.reshape(owner_count * block_count, per_owner, column_count),
        "fsdp",
        split_axis=0,
        concat_axis=0,
        tiled=True,
    ).reshape(row_count, column_count)
    new_rollout = wide(rollout, incoming).astype(jnp.bfloat16)
    return (new_master, new_one, new_two, new_amax, new_rollout)


def solution(mesh):
    return jax.shard_map(
        body,
        mesh=mesh,
        in_specs=(
            P("dp", "fsdp", None),
            P("fsdp", "dp"),
            P("fsdp", "dp"),
            P("fsdp", "dp"),
            P("fsdp", "dp"),
            P("fsdp", "dp"),
            P("fsdp", "dp"),
            P(),
            P(),
        ),
        out_specs=(
            P("fsdp", "dp"),
            P("fsdp", "dp"),
            P("fsdp", "dp"),
            P("fsdp", "dp"),
            P("fsdp", "dp"),
        ),
        check_vma=False,
    )
```

```python
import functools

import jax
import jax.numpy as jnp
from jax import lax
from jax.experimental import pallas as pl
from jax.experimental.pallas import tpu as pltpu
from jax.sharding import PartitionSpec as P

D = 7168
TILE = 128
CHUNKS = 2

beta_one = 0.9
beta_two = 0.95
bias_one = 1.0 - 0.9**10
bias_two = 1.0 - 0.95**10
step_size = 0.05
weight_decay = 0.1
adam_floor = 1e-08

VMEM = pl.BlockSpec(memory_space=pltpu.VMEM)
ANY = pl.BlockSpec(memory_space=pl.ANY)
SMEM = pl.BlockSpec(memory_space=pltpu.SMEM)


def adam_step(master, moment_one, moment_two, gradient):
    new_one = beta_one * moment_one + (1.0 - beta_one) * gradient
    new_two = beta_two * moment_two + (1.0 - beta_two) * gradient * gradient
    update = new_one / bias_one / (jnp.sqrt(new_two / bias_two) + adam_floor)
    new_master = master - step_size * (update + weight_decay * master)
    return (new_master, new_one, new_two)


def exchange(x, bit, replica_count):
    return lax.ppermute(x, "dp", [(i, i ^ (1 << bit)) for i in range(replica_count)])


def partial_sum(block, first_row, rows, own, core, later):
    columns = pl.ds(pl.multiple_of(block * TILE, TILE), TILE)
    total = own[block >> 1, pl.ds(first_row, rows)].astype(jnp.float32)
    total = total + core[0, pl.ds(first_row, rows), columns].astype(jnp.float32)
    for step, received in enumerate(later):
        total = total + received[block >> (step + 2)].astype(jnp.float32)
    return total


def keeping_kernel(gradients, out, arrived):
    core = lax.axis_index("dp") & 1
    copies = []
    for q in range(out.shape[0]):
        columns = pl.ds(pl.multiple_of((2 * q + core) * TILE, TILE), TILE)
        copy = pltpu.make_async_copy(gradients.at[0, :, columns], out.at[q], arrived.at[q])
        copy.start()
        copies.append(copy)
    for copy in copies:
        copy.wait()


def keeping(gradients, replica_count):
    count, row_count = replica_count // 2, gradients.shape[1]
    return pl.pallas_call(
        keeping_kernel,
        out_shape=jax.ShapeDtypeStruct((count, row_count, TILE), jnp.bfloat16),
        in_specs=[ANY],
        out_specs=VMEM,
        scratch_shapes=[pltpu.SemaphoreType.DMA((count,))],
        compiler_params=pltpu.CompilerParams(vmem_limit_bytes=16 * 2**20),
        cost_estimate=pl.CostEstimate(
            flops=0, bytes_accessed=4 * count * row_count * TILE, transcendentals=0
        ),
    )(gradients)


def sending_kernel(bit, first_row, own, core, *rest):
    later, out = rest[:-1], rest[-1]
    place = lax.axis_index("dp")
    low = place & ((1 << bit) - 1)
    other = (1 - ((place >> bit) & 1)) << bit
    for q in range(out.shape[0]):
        block = (q << (bit + 1)) | other | low
        out[q] = partial_sum(block, first_row, out.shape[1], own, core, later).astype(out.dtype)


def sending(bit, first_row, rows, replica_count, own, core, later):
    shape = (replica_count >> (bit + 1), rows, TILE)
    return pl.pallas_call(
        functools.partial(sending_kernel, bit, first_row),
        out_shape=jax.ShapeDtypeStruct(shape, jnp.bfloat16),
        in_specs=[VMEM] * (2 + len(later)),
        out_specs=VMEM,
        compiler_params=pltpu.CompilerParams(vmem_limit_bytes=16 * 2**20),
        cost_estimate=pl.CostEstimate(
            flops=3 * shape[0] * rows * TILE, bytes_accessed=6 * shape[0] * rows * TILE, transcendentals=0
        ),
    )(own, core, *later)


def step_kernel(
    steps, replica_count, own, core, *rest
):
    later = rest[: steps * CHUNKS]
    master, one, two, synced, record, chooser = rest[steps * CHUNKS : steps * CHUNKS + 6]
    new_master, new_one, new_two, column_max, outgoing, clipped = rest[steps * CHUNKS + 6 :]
    place = lax.axis_index("dp")
    row_count = master.shape[0]
    rows = row_count // CHUNKS
    piece = TILE // 2
    for r in range(row_count // piece):
        at = pl.ds(r * piece, piece)
        columns = pl.ds(pl.multiple_of(place * TILE, TILE), TILE)
        total = own[place >> 1, at].astype(jnp.float32) + core[0, at, columns].astype(jnp.float32)
        chunk = r * piece // rows
        inner = pl.ds(r * piece - chunk * rows, piece)
        for step in range(steps):
            received = later[chunk * steps + step]
            total = total + received[place >> (step + 2), inner].astype(jnp.float32)
        a, b, c = adam_step(master[at], one[at], two[at], total / replica_count)
        new_master[at] = a
        new_one[at] = b
        new_two[at] = c
        delta = a - synced[at].astype(jnp.float32)
        tile = r * piece // TILE
        peak = jnp.max(jnp.abs(delta), axis=0, keepdims=True)
        if r * piece % TILE == 0:
            column_max[pl.ds(tile, 1)] = peak
        else:
            column_max[pl.ds(tile, 1)] = jnp.maximum(column_max[pl.ds(tile, 1)], peak)
        limit = record[0, tile]
        clipped[at] = jnp.clip(delta, -limit, limit).astype(jnp.bfloat16)
    outgoing[...] = jnp.dot(
        chooser[...], clipped[...], preferred_element_type=jnp.float32
    ).astype(jnp.bfloat16)


def body(
    gradients, master, moment_one, moment_two, synced, rollout, amax_record, row_table, expert_owner
):
    owner_count = lax.axis_size("fsdp")
    replica_count = lax.axis_size("dp")
    row_count, column_count = master.shape
    block_count = row_count // TILE
    per_owner = TILE // owner_count

    core = exchange(gradients, 0, replica_count)
    own = keeping(gradients, replica_count)
    rows = row_count // CHUNKS
    later = [[] for _ in range(CHUNKS)]
    steps = replica_count.bit_length() - 2
    for bit in range(1, steps + 1):
        for chunk in range(CHUNKS):
            out = sending(bit, chunk * rows, rows, replica_count, own, core, later[chunk])
            later[chunk].append(exchange(out, bit, replica_count))

    index = jnp.arange(TILE, dtype=jnp.int32)
    before = (row_table[None, :] < row_table[:, None]) | (
        (row_table[None, :] == row_table[:, None]) & (index[None, :] < index[:, None])
    )
    rank = jnp.sum(before.astype(jnp.int32), axis=1)
    blocks = jnp.arange(block_count, dtype=jnp.int32)
    experts = (lax.axis_index("fsdp") * block_count + blocks) * TILE // D
    shifts = expert_owner[experts]
    owner = (rank[None, :] // per_owner + shifts[:, None]) % owner_count
    slot = (owner * block_count + blocks[:, None]) * per_owner + rank[None, :] % per_owner
    chooser = (
        jnp.arange(row_count, dtype=jnp.int32)[:, None] == slot.reshape(1, row_count)
    ).astype(jnp.bfloat16)

    full = jax.ShapeDtypeStruct(master.shape, jnp.float32)
    new_master, new_one, new_two, column_max, outgoing = pl.pallas_call(
        functools.partial(step_kernel, steps, replica_count),
        out_shape=(
            full,
            full,
            full,
            jax.ShapeDtypeStruct((block_count, TILE), jnp.float32),
            jax.ShapeDtypeStruct(master.shape, jnp.bfloat16),
        ),
        in_specs=[VMEM] * (2 + steps * CHUNKS + 4) + [SMEM, VMEM],
        out_specs=(VMEM,) * 5,
        scratch_shapes=[pltpu.VMEM(master.shape, jnp.bfloat16)],
        compiler_params=pltpu.CompilerParams(vmem_limit_bytes=16 * 2**20),
    )(
        own,
        core,
        *[x for group in later for x in group],
        master,
        moment_one,
        moment_two,
        synced,
        amax_record.reshape(1, block_count),
        chooser,
    )
    new_amax = jnp.max(column_max, axis=1).reshape(block_count, 1)
    incoming = lax.all_to_all(
        outgoing.reshape(owner_count * block_count, per_owner, column_count),
        "fsdp",
        split_axis=0,
        concat_axis=0,
        tiled=True,
    ).reshape(row_count, column_count)
    new_rollout = (rollout.astype(jnp.float32) + incoming.astype(jnp.float32)).astype(jnp.bfloat16)
    return (new_master, new_one, new_two, new_amax, new_rollout)


def solution(mesh):
    return jax.shard_map(
        body,
        mesh=mesh,
        in_specs=(
            P("dp", "fsdp", None),
            P("fsdp", "dp"),
            P("fsdp", "dp"),
            P("fsdp", "dp"),
            P("fsdp", "dp"),
            P("fsdp", "dp"),
            P("fsdp", "dp"),
            P(),
            P(),
        ),
        out_specs=(
            P("fsdp", "dp"),
            P("fsdp", "dp"),
            P("fsdp", "dp"),
            P("fsdp", "dp"),
            P("fsdp", "dp"),
        ),
        check_vma=False,
    )
```

```python
import functools

import jax
import jax.numpy as jnp
from jax import lax
from jax.experimental import pallas as pl
from jax.experimental.pallas import tpu as pltpu
from jax.sharding import PartitionSpec as P

D = 7168
TILE = 128
HALF = TILE // 2

beta_one = 0.9
beta_two = 0.95
bias_one = 1.0 - 0.9**10
bias_two = 1.0 - 0.95**10
step_size = 0.05
weight_decay = 0.1
adam_floor = 1e-08

VMEM = pl.BlockSpec(memory_space=pltpu.VMEM)
SMEM = pl.BlockSpec(memory_space=pltpu.SMEM)
ANY = pl.BlockSpec(memory_space=pl.ANY)
F32 = jnp.float32
BF16 = jnp.bfloat16


def adam_step(master, moment_one, moment_two, gradient):
    new_one = beta_one * moment_one + (1.0 - beta_one) * gradient
    new_two = beta_two * moment_two + (1.0 - beta_two) * gradient * gradient
    update = new_one / bias_one / (jnp.sqrt(new_two / bias_two) + adam_floor)
    new_master = master - step_size * (update + weight_decay * master)
    return (new_master, new_one, new_two)


def call(kernel, outs, ins, args, scratch=(), bytes_accessed=2**20):
    single = not isinstance(outs, (tuple, list))
    return pl.pallas_call(
        kernel,
        out_shape=outs,
        in_specs=ins,
        out_specs=VMEM if single else (VMEM,) * len(outs),
        scratch_shapes=list(scratch),
        compiler_params=pltpu.CompilerParams(vmem_limit_bytes=16 * 2**20),
        cost_estimate=pl.CostEstimate(
            flops=bytes_accessed, bytes_accessed=bytes_accessed, transcendentals=0
        ),
    )(*args)


def exchange(x, axis, distance, count):
    return lax.ppermute(x, axis, [(i, i ^ distance) for i in range(count)])


def ranks(across, down, axis):
    i = lax.broadcasted_iota(jnp.int32, (TILE, TILE), 1 - axis)
    j = lax.broadcasted_iota(jnp.int32, (TILE, TILE), axis)
    mine, other = (across, down) if axis == 0 else (down, across)
    before = (other < mine) | ((other == mine) & (j < i))
    return jnp.sum(before.astype(jnp.int32), axis=axis, keepdims=True)


def owners_of(rank, block, expert_owner, owner_count, block_count):
    per_owner = TILE // owner_count
    expert = (lax.axis_index("fsdp") * block_count + block) * TILE // D
    turned = rank // per_owner + expert_owner[expert]
    owner = jnp.where(turned >= owner_count, turned - owner_count, turned)
    half = owner_count // 2
    top = (owner >= half).astype(jnp.int32)
    inner = owner - top * half
    here = (lax.axis_index("fsdp") >= half).astype(jnp.int32)
    stays = (top == here).astype(jnp.int32)
    pair = rank - rank // per_owner * per_owner
    return inner, pair, stays, here


def picking_kernel(owner_count, across, down, expert_owner, picks):
    per_owner = TILE // owner_count
    block_count = picks.shape[0] // TILE
    rank = ranks(across[...], down[...], 0)
    place = lax.broadcasted_iota(jnp.int32, (HALF, TILE), 0)
    for block in range(block_count):
        inner, pair, stays, _ = owners_of(rank, block, expert_owner, owner_count, block_count)
        slot = inner * per_owner + pair + stays * HALF
        for chunk in range(2):
            at = (chunk * block_count + block) * HALF
            picks[pl.ds(at, HALF)] = (place + chunk * HALF == slot).astype(F32).astype(BF16)


def placing_kernel(owner_count, across, down, expert_owner, back_go, back_stay, pick_go, pack_stay):
    per_owner = TILE // owner_count
    row_count = back_go.shape[0]
    block_count = row_count // TILE
    chunk_rows = row_count // 2
    along = ranks(across[...], down[...], 0)
    upright = ranks(across[...], down[...], 1)
    lanes = lax.broadcasted_iota(jnp.int32, (TILE, chunk_rows), 1)
    sublanes = lax.broadcasted_iota(jnp.int32, (row_count, TILE), 0)
    for block in range(block_count):
        at = pl.ds(block * TILE, TILE)
        inner, pair, stays, _ = owners_of(upright, block, expert_owner, owner_count, block_count)
        slot = block * HALF + inner * per_owner + pair
        back_go[at] = (lanes == jnp.where(stays == 0, slot, -1)).astype(F32).astype(BF16)
        back_stay[at] = (lanes == jnp.where(stays == 1, slot, -1)).astype(F32).astype(BF16)
        inner, pair, stays, here = owners_of(along, block, expert_owner, owner_count, block_count)
        slot = block * HALF + inner * per_owner + pair
        pick_go[:, at] = (
            (sublanes[:chunk_rows] == jnp.where(stays == 0, slot, -1)).astype(F32).astype(BF16)
        )
        sent = ((inner * 2 + here) * block_count + block) * per_owner + pair
        pack_stay[:, at] = (sublanes == jnp.where(stays == 1, sent, -1)).astype(F32).astype(BF16)


def keeping_kernel(gradients, out, arrived):
    core = lax.axis_index("dp") & 1
    copies = []
    for q in range(out.shape[0]):
        columns = pl.ds(pl.multiple_of((2 * q + core) * TILE, TILE), TILE)
        copy = pltpu.make_async_copy(gradients.at[0, :, columns], out.at[q], arrived.at[q])
        copy.start()
        copies.append(copy)
    for copy in copies:
        copy.wait()


def first_kernel(sent, chunks, own, core, picks, out):
    place = lax.axis_index("dp")
    count, block_count = out.shape[0], own.shape[1] // TILE
    bit = (place >> 1) & 1
    wanted = (1 - bit) if sent else bit
    for r in range(block_count):
        at = pl.ds(r * TILE, TILE)
        sums = []
        for q in range(count):
            block = (q << 2) | (wanted << 1) | (place & 1)
            columns = pl.ds(pl.multiple_of(block * TILE, TILE), TILE)
            sums.append((own[block >> 1, at].astype(F32) + core[0, at, columns].astype(F32)).astype(BF16))
        joined = jnp.concatenate(sums, axis=1)
        for n, chunk in enumerate(chunks):
            pick = picks[pl.ds((chunk * block_count + r) * HALF, HALF)]
            moved = jnp.dot(pick, joined, preferred_element_type=F32).astype(BF16)
            for q in range(count):
                out[q, pl.ds((n * block_count + r) * HALF, HALF)] = moved[:, q * TILE : (q + 1) * TILE]


def sum_so_far(block, chunk, kept, later):
    rows = later[0].shape[1]
    total = kept[block >> 2, pl.ds(chunk * rows, rows)].astype(F32)
    for step, received in enumerate(later):
        total = total + received[block >> (step + 2)].astype(F32)
    return total


def sending_kernel(bit, chunk, kept, *rest):
    later, out = rest[:-1], rest[-1]
    place = lax.axis_index("dp")
    low = place & ((1 << bit) - 1)
    other = (1 - ((place >> bit) & 1)) << bit
    for q in range(out.shape[0]):
        block = (q << (bit + 1)) | other | low
        out[q] = sum_so_far(block, chunk, kept, later).astype(BF16)


def in_two(total, parts):
    high = total.astype(BF16)
    parts[:, :TILE] = high
    parts[:, TILE:] = (total - high.astype(F32)).astype(BF16)


def going_kernel(steps, replica_count, kept, *rest):
    later = rest[:steps]
    master, one, two, synced, record, back, pick, summed, outgoing, parts, clipped = rest[steps:]
    in_two(sum_so_far(lax.axis_index("dp"), 0, kept, later), parts)
    for tile in range(master.shape[0] // TILE):
        at = pl.ds(tile * TILE, TILE)
        pieces = jnp.dot(back[at], parts[...], preferred_element_type=F32)
        total = pieces[:, :TILE] + pieces[:, TILE:]
        summed[at] = total
        updated, _, _ = adam_step(master[at], one[at], two[at], total / replica_count)
        delta = updated - synced[at].astype(F32)
        limit = record[0, tile]
        clipped[at] = jnp.clip(delta, -limit, limit).astype(BF16)
    outgoing[...] = jnp.dot(pick[...], clipped[...], preferred_element_type=F32).astype(BF16)


def staying_kernel(steps, replica_count, kept, *rest):
    later = rest[:steps]
    master, one, two, synced, record, back, pack, summed = rest[steps : steps + 8]
    new_master, new_one, new_two, column_max, packed, parts, clipped = rest[steps + 8 :]
    in_two(sum_so_far(lax.axis_index("dp"), 1, kept, later), parts)
    for tile in range(master.shape[0] // TILE):
        at = pl.ds(tile * TILE, TILE)
        pieces = jnp.dot(back[at], parts[...], preferred_element_type=F32)
        total = summed[at] + (pieces[:, :TILE] + pieces[:, TILE:])
        a, b, c = adam_step(master[at], one[at], two[at], total / replica_count)
        new_master[at] = a
        new_one[at] = b
        new_two[at] = c
        delta = a - synced[at].astype(F32)
        column_max[pl.ds(tile, 1)] = jnp.max(jnp.abs(delta), axis=0, keepdims=True)
        limit = record[0, tile]
        clipped[at] = jnp.clip(delta, -limit, limit).astype(BF16)
    packed[...] = jnp.dot(pack[...], clipped[...], preferred_element_type=F32).astype(BF16)


def packing_kernel(owner_count, arrived, staying, out):
    per_owner = TILE // owner_count
    half = owner_count // 2
    row_count, chunk_rows = out.shape[0], arrived.shape[0]
    block_count = row_count // TILE
    there = 1 - (lax.axis_index("fsdp") >= half).astype(jnp.int32)
    row = lax.broadcasted_iota(jnp.int32, (1, chunk_rows), 1)
    block = row // HALF
    inner = (row - block * HALF) // per_owner
    pair = row - row // per_owner * per_owner
    sent = ((inner * 2 + there) * block_count + block) * per_owner + pair
    pack = (lax.broadcasted_iota(jnp.int32, (row_count, chunk_rows), 0) == sent).astype(F32).astype(BF16)
    moved = jnp.dot(pack, arrived[...], preferred_element_type=F32)
    out[...] = (moved + staying[...].astype(F32)).astype(BF16)


def adding_kernel(owner_count, incoming, rollout, out):
    group = rollout.shape[0] // owner_count
    half = owner_count // 2
    row_count = rollout.shape[0]
    row = lax.broadcasted_iota(jnp.int32, (1, row_count), 1)
    source = row // group
    wanted = ((source & 1) * half + (source >> 1)) * group + (row - source * group)
    order = (lax.broadcasted_iota(jnp.int32, (row_count, row_count), 0) == wanted).astype(F32).astype(BF16)
    moved = jnp.dot(order, incoming[...], preferred_element_type=F32)
    out[...] = (rollout[...].astype(F32) + moved).astype(BF16)


def body(
    gradients, master, moment_one, moment_two, synced, rollout, amax_record, row_table, expert_owner
):
    owner_count = lax.axis_size("fsdp")
    replica_count = lax.axis_size("dp")
    row_count, column_count = master.shape
    block_count = row_count // TILE
    rows = row_count // 2
    half = owner_count // 2

    def shape(*dims, dtype=BF16):
        return jax.ShapeDtypeStruct(dims, dtype)

    core = exchange(gradients, "dp", 1, replica_count)
    own = call(
        keeping_kernel,
        shape(replica_count // 2, row_count, TILE),
        [ANY],
        [gradients],
        [pltpu.SemaphoreType.DMA((replica_count // 2,))],
    )
    table = [row_table.reshape(1, TILE), row_table.reshape(TILE, 1), expert_owner]
    table_specs = [VMEM, VMEM, SMEM]
    picks = call(
        functools.partial(picking_kernel, owner_count), shape(row_count, TILE), table_specs, table
    )

    later = [[], []]
    steps = replica_count.bit_length() - 2
    for chunk in range(2):
        out = call(
            functools.partial(first_kernel, True, (chunk,)),
            shape(replica_count // 4, rows, TILE),
            [VMEM] * 3,
            [own, core, picks],
        )
        later[chunk].append(exchange(out, "dp", 2, replica_count))
    kept = call(
        functools.partial(first_kernel, False, (0, 1)),
        shape(replica_count // 4, row_count, TILE),
        [VMEM] * 3,
        [own, core, picks],
    )
    back_go, back_stay, pick_go, pack_stay = call(
        functools.partial(placing_kernel, owner_count),
        (
            shape(row_count, rows),
            shape(row_count, rows),
            shape(rows, row_count),
            shape(row_count, row_count),
        ),
        table_specs,
        table,
    )
    for bit in range(2, steps + 1):
        for chunk in range(2):
            out = call(
                functools.partial(sending_kernel, bit, chunk),
                shape(replica_count >> (bit + 1), rows, TILE),
                [VMEM] * (1 + len(later[chunk])),
                [kept, *later[chunk]],
            )
            later[chunk].append(exchange(out, "dp", 1 << bit, replica_count))

    state = [master, moment_one, moment_two, synced, amax_record.reshape(1, block_count)]
    state_specs = [VMEM] * 4 + [SMEM]
    scratch = [pltpu.VMEM((rows, 2 * TILE), BF16), pltpu.VMEM((row_count, TILE), BF16)]
    summed, outgoing = call(
        functools.partial(going_kernel, steps, replica_count),
        (shape(row_count, TILE, dtype=F32), shape(rows, TILE)),
        [VMEM] * (1 + steps) + state_specs + [VMEM] * 2,
        [kept, *later[0], *state, back_go, pick_go],
        scratch,
    )
    arrived = exchange(outgoing, "fsdp", half, owner_count)
    full = shape(row_count, TILE, dtype=F32)
    new_master, new_one, new_two, column_max, packed = call(
        functools.partial(staying_kernel, steps, replica_count),
        (full, full, full, shape(block_count, TILE, dtype=F32), shape(row_count, TILE)),
        [VMEM] * (1 + steps) + state_specs + [VMEM] * 3,
        [kept, *later[1], *state, back_stay, pack_stay, summed],
        scratch,
    )
    new_amax = jnp.max(column_max, axis=1).reshape(block_count, 1)
    packed = call(
        functools.partial(packing_kernel, owner_count),
        shape(row_count, TILE),
        [VMEM] * 2,
        [arrived, packed],
    )
    incoming = lax.all_to_all(
        packed.reshape(row_count // 2, 2, TILE),
        "fsdp",
        split_axis=0,
        concat_axis=0,
        axis_index_groups=[list(range(half)), list(range(half, owner_count))],
        tiled=True,
    ).reshape(row_count, TILE)
    new_rollout = call(
        functools.partial(adding_kernel, owner_count),
        shape(row_count, TILE),
        [VMEM] * 2,
        [incoming, rollout],
    )
    return (new_master, new_one, new_two, new_amax, new_rollout)


def solution(mesh):
    return jax.shard_map(
        body,
        mesh=mesh,
        in_specs=(
            P("dp", "fsdp", None),
            P("fsdp", "dp"),
            P("fsdp", "dp"),
            P("fsdp", "dp"),
            P("fsdp", "dp"),
            P("fsdp", "dp"),
            P("fsdp", "dp"),
            P(),
            P(),
        ),
        out_specs=(
            P("fsdp", "dp"),
            P("fsdp", "dp"),
            P("fsdp", "dp"),
            P("fsdp", "dp"),
            P("fsdp", "dp"),
        ),
        check_vma=False,
    )
```

```python
import functools

import jax
import jax.numpy as jnp
from jax import lax
from jax.experimental import pallas as pl
from jax.experimental.pallas import tpu as pltpu
from jax.sharding import PartitionSpec as P

D = 7168
TILE = 128
HALF = TILE // 2

beta_one = 0.9
beta_two = 0.95
bias_one = 1.0 - 0.9**10
bias_two = 1.0 - 0.95**10
step_size = 0.05
weight_decay = 0.1
adam_floor = 1e-08

VMEM = pl.BlockSpec(memory_space=pltpu.VMEM)
SMEM = pl.BlockSpec(memory_space=pltpu.SMEM)
ANY = pl.BlockSpec(memory_space=pl.ANY)
F32 = jnp.float32
BF16 = jnp.bfloat16


def adam_step(master, moment_one, moment_two, gradient):
    new_one = beta_one * moment_one + (1.0 - beta_one) * gradient
    new_two = beta_two * moment_two + (1.0 - beta_two) * gradient * gradient
    update = new_one / bias_one / (jnp.sqrt(new_two / bias_two) + adam_floor)
    new_master = master - step_size * (update + weight_decay * master)
    return (new_master, new_one, new_two)


def call(kernel, outs, ins, args, scratch=(), bytes_accessed=2**20):
    single = not isinstance(outs, (tuple, list))
    return pl.pallas_call(
        kernel,
        out_shape=outs,
        in_specs=ins,
        out_specs=VMEM if single else (VMEM,) * len(outs),
        scratch_shapes=list(scratch),
        compiler_params=pltpu.CompilerParams(vmem_limit_bytes=16 * 2**20),
        cost_estimate=pl.CostEstimate(
            flops=bytes_accessed, bytes_accessed=bytes_accessed, transcendentals=0
        ),
    )(*args)


def exchange(x, axis, distance, count):
    return lax.ppermute(x, axis, [(i, i ^ distance) for i in range(count)])


def ranks(across, down, axis):
    i = lax.broadcasted_iota(jnp.int32, (TILE, TILE), 1 - axis)
    j = lax.broadcasted_iota(jnp.int32, (TILE, TILE), axis)
    mine, other = (across, down) if axis == 0 else (down, across)
    before = (other < mine) | ((other == mine) & (j < i))
    return jnp.sum(before.astype(jnp.int32), axis=axis, keepdims=True)


def owners_of(rank, block, expert_owner, owner_count, block_count):
    per_owner = TILE // owner_count
    expert = (lax.axis_index("fsdp") * block_count + block) * TILE // D
    turned = rank // per_owner + expert_owner[expert]
    owner = jnp.where(turned >= owner_count, turned - owner_count, turned)
    half = owner_count // 2
    top = (owner >= half).astype(jnp.int32)
    inner = owner - top * half
    here = (lax.axis_index("fsdp") >= half).astype(jnp.int32)
    stays = (top == here).astype(jnp.int32)
    pair = rank - rank // per_owner * per_owner
    return inner, pair, stays, here


def picking_kernel(owner_count, across, down, expert_owner, picks):
    per_owner = TILE // owner_count
    block_count = picks.shape[0] // TILE
    rank = ranks(across[...], down[...], 0)
    place = lax.broadcasted_iota(jnp.int32, (HALF, TILE), 0)
    for block in range(block_count):
        inner, pair, stays, _ = owners_of(rank, block, expert_owner, owner_count, block_count)
        slot = inner * per_owner + pair + stays * HALF
        for chunk in range(2):
            at = (chunk * block_count + block) * HALF
            picks[pl.ds(at, HALF)] = (place + chunk * HALF == slot).astype(F32).astype(BF16)


def placing_kernel(
    owner_count,
    across,
    down,
    expert_owner,
    core,
    back_go,
    back_stay,
    pick_go,
    pack_stay,
    pack_go,
    order,
):
    del core
    per_owner = TILE // owner_count
    row_count = back_go.shape[0]
    block_count = row_count // TILE
    chunk_rows = row_count // 2
    along = ranks(across[...], down[...], 0)
    upright = ranks(across[...], down[...], 1)
    lanes = lax.broadcasted_iota(jnp.int32, (TILE, chunk_rows), 1)
    sublanes = lax.broadcasted_iota(jnp.int32, (row_count, TILE), 0)
    for block in range(block_count):
        at = pl.ds(block * TILE, TILE)
        inner, pair, stays, _ = owners_of(upright, block, expert_owner, owner_count, block_count)
        slot = block * HALF + inner * per_owner + pair
        back_go[at] = (lanes == jnp.where(stays == 0, slot, -1)).astype(F32).astype(BF16)
        back_stay[at] = (lanes == jnp.where(stays == 1, slot, -1)).astype(F32).astype(BF16)
        inner, pair, stays, here = owners_of(along, block, expert_owner, owner_count, block_count)
        slot = block * HALF + inner * per_owner + pair
        pick_go[:, at] = (
            (sublanes[:chunk_rows] == jnp.where(stays == 0, slot, -1)).astype(F32).astype(BF16)
        )
        sent = ((inner * 2 + here) * block_count + block) * per_owner + pair
        pack_stay[:, at] = (sublanes == jnp.where(stays == 1, sent, -1)).astype(F32).astype(BF16)

    half = owner_count // 2
    there = 1 - (lax.axis_index("fsdp") >= half).astype(jnp.int32)
    row = lax.broadcasted_iota(jnp.int32, (1, chunk_rows), 1)
    block = row // HALF
    inner = (row - block * HALF) // per_owner
    pair = row - row // per_owner * per_owner
    sent = ((inner * 2 + there) * block_count + block) * per_owner + pair
    pack_go[...] = (
        (lax.broadcasted_iota(jnp.int32, (row_count, chunk_rows), 0) == sent).astype(F32).astype(BF16)
    )

    group = block_count * per_owner
    row = lax.broadcasted_iota(jnp.int32, (1, row_count), 1)
    source = row // group
    wanted = ((source & 1) * half + (source >> 1)) * group + (row - source * group)
    order[...] = (
        (lax.broadcasted_iota(jnp.int32, (row_count, row_count), 0) == wanted).astype(F32).astype(BF16)
    )


def keeping_kernel(gradients, out, arrived):
    core = lax.axis_index("dp") & 1
    copies = []
    for q in range(out.shape[0]):
        columns = pl.ds(pl.multiple_of((2 * q + core) * TILE, TILE), TILE)
        copy = pltpu.make_async_copy(gradients.at[0, :, columns], out.at[q], arrived.at[q])
        copy.start()
        copies.append(copy)
    for copy in copies:
        copy.wait()


def first_kernel(sent, chunks, own, core, picks, *rest):
    out = rest[-1]
    place = lax.axis_index("dp")
    count, block_count = out.shape[0], own.shape[1] // TILE
    bit = (place >> 1) & 1
    wanted = (1 - bit) if sent else bit
    for r in range(block_count):
        at = pl.ds(r * TILE, TILE)
        sums = []
        for q in range(count):
            block = (q << 2) | (wanted << 1) | (place & 1)
            columns = pl.ds(pl.multiple_of(block * TILE, TILE), TILE)
            sums.append((own[block >> 1, at].astype(F32) + core[0, at, columns].astype(F32)).astype(BF16))
        joined = jnp.concatenate(sums, axis=1)
        for n, chunk in enumerate(chunks):
            pick = picks[pl.ds((chunk * block_count + r) * HALF, HALF)]
            moved = jnp.dot(pick, joined, preferred_element_type=F32).astype(BF16)
            for q in range(count):
                out[q, pl.ds((n * block_count + r) * HALF, HALF)] = moved[:, q * TILE : (q + 1) * TILE]


def sum_so_far(block, chunk, kept, later):
    rows = later[0].shape[1]
    total = kept[block >> 2, pl.ds(chunk * rows, rows)].astype(F32)
    for step, received in enumerate(later):
        total = total + received[block >> (step + 2)].astype(F32)
    return total


def sending_kernel(bit, chunk, kept, *rest):
    later, out = rest[:-1], rest[-1]
    place = lax.axis_index("dp")
    low = place & ((1 << bit) - 1)
    other = (1 - ((place >> bit) & 1)) << bit
    for q in range(out.shape[0]):
        block = (q << (bit + 1)) | other | low
        out[q] = sum_so_far(block, chunk, kept, later).astype(BF16)


def in_two(total, parts):
    high = total.astype(BF16)
    parts[:, :TILE] = high
    parts[:, TILE:] = (total - high.astype(F32)).astype(BF16)


def going_kernel(steps, replica_count, kept, *rest):
    later = rest[:steps]
    master, one, two, synced, record, back, pick, summed, outgoing, parts, clipped = rest[steps:]
    in_two(sum_so_far(lax.axis_index("dp"), 0, kept, later), parts)
    for tile in range(master.shape[0] // TILE):
        at = pl.ds(tile * TILE, TILE)
        pieces = jnp.dot(back[at], parts[...], preferred_element_type=F32)
        total = pieces[:, :TILE] + pieces[:, TILE:]
        summed[at] = total
        updated, _, _ = adam_step(master[at], one[at], two[at], total / replica_count)
        delta = updated - synced[at].astype(F32)
        limit = record[0, tile]
        clipped[at] = jnp.clip(delta, -limit, limit).astype(BF16)
    outgoing[...] = jnp.dot(pick[...], clipped[...], preferred_element_type=F32).astype(BF16)


def staying_kernel(steps, replica_count, kept, *rest):
    later = rest[:steps]
    master, one, two, synced, record, back, pack, summed = rest[steps : steps + 8]
    new_master, new_one, new_two, column_max, packed, parts, clipped = rest[steps + 8 :]
    in_two(sum_so_far(lax.axis_index("dp"), 1, kept, later), parts)
    for tile in range(master.shape[0] // TILE):
        at = pl.ds(tile * TILE, TILE)
        pieces = jnp.dot(back[at], parts[...], preferred_element_type=F32)
        total = summed[at] + (pieces[:, :TILE] + pieces[:, TILE:])
        a, b, c = adam_step(master[at], one[at], two[at], total / replica_count)
        new_master[at] = a
        new_one[at] = b
        new_two[at] = c
        delta = a - synced[at].astype(F32)
        column_max[pl.ds(tile, 1)] = jnp.max(jnp.abs(delta), axis=0, keepdims=True)
        limit = record[0, tile]
        clipped[at] = jnp.clip(delta, -limit, limit).astype(BF16)
    packed[...] = jnp.dot(pack[...], clipped[...], preferred_element_type=F32).astype(BF16)


def packing_kernel(arrived, pack, staying, out):
    moved = jnp.dot(pack[...], arrived[...], preferred_element_type=F32)
    out[...] = (moved + staying[...].astype(F32)).astype(BF16)


def adding_kernel(incoming, order, rollout, out):
    moved = jnp.dot(order[...], incoming[...], preferred_element_type=F32)
    out[...] = (rollout[...].astype(F32) + moved).astype(BF16)


def body(
    gradients, master, moment_one, moment_two, synced, rollout, amax_record, row_table, expert_owner
):
    owner_count = lax.axis_size("fsdp")
    replica_count = lax.axis_size("dp")
    row_count, column_count = master.shape
    block_count = row_count // TILE
    rows = row_count // 2
    half = owner_count // 2

    def shape(*dims, dtype=BF16):
        return jax.ShapeDtypeStruct(dims, dtype)

    core = exchange(gradients, "dp", 1, replica_count)
    own = call(
        keeping_kernel,
        shape(replica_count // 2, row_count, TILE),
        [ANY],
        [gradients],
        [pltpu.SemaphoreType.DMA((replica_count // 2,))],
    )
    table = [row_table.reshape(1, TILE), row_table.reshape(TILE, 1), expert_owner]
    table_specs = [VMEM, VMEM, SMEM]
    picks = call(
        functools.partial(picking_kernel, owner_count), shape(row_count, TILE), table_specs, table
    )

    later = [[], []]
    steps = replica_count.bit_length() - 2
    sent = shape(replica_count // 4, rows, TILE)
    summands = [own, core, picks]
    first = call(functools.partial(first_kernel, True, (0,)), sent, [VMEM] * 3, summands)
    later[0].append(exchange(first, "dp", 2, replica_count))
    kept = call(
        functools.partial(first_kernel, False, (0, 1)),
        shape(replica_count // 4, row_count, TILE),
        [VMEM] * 3,
        summands,
    )
    back_go, back_stay, pick_go, pack_stay, pack_go, order = call(
        functools.partial(placing_kernel, owner_count),
        (
            shape(row_count, rows),
            shape(row_count, rows),
            shape(rows, row_count),
            shape(row_count, row_count),
            shape(row_count, rows),
            shape(row_count, row_count),
        ),
        [*table_specs, ANY],
        [*table, core],
    )
    second = call(
        functools.partial(first_kernel, True, (1,)),
        sent,
        [VMEM] * 3 + [ANY] * 2,
        [*summands, kept, pick_go],
    )
    later[1].append(exchange(second, "dp", 2, replica_count))
    for bit in range(2, steps + 1):
        for chunk in range(2):
            out = call(
                functools.partial(sending_kernel, bit, chunk),
                shape(replica_count >> (bit + 1), rows, TILE),
                [VMEM] * (1 + len(later[chunk])),
                [kept, *later[chunk]],
            )
            later[chunk].append(exchange(out, "dp", 1 << bit, replica_count))

    state = [master, moment_one, moment_two, synced, amax_record.reshape(1, block_count)]
    state_specs = [VMEM] * 4 + [SMEM]
    scratch = [pltpu.VMEM((rows, 2 * TILE), BF16), pltpu.VMEM((row_count, TILE), BF16)]
    summed, outgoing = call(
        functools.partial(going_kernel, steps, replica_count),
        (shape(row_count, TILE, dtype=F32), shape(rows, TILE)),
        [VMEM] * (1 + steps) + state_specs + [VMEM] * 2,
        [kept, *later[0], *state, back_go, pick_go],
        scratch,
    )
    arrived = exchange(outgoing, "fsdp", half, owner_count)
    full = shape(row_count, TILE, dtype=F32)
    new_master, new_one, new_two, column_max, packed = call(
        functools.partial(staying_kernel, steps, replica_count),
        (full, full, full, shape(block_count, TILE, dtype=F32), shape(row_count, TILE)),
        [VMEM] * (1 + steps) + state_specs + [VMEM] * 3,
        [kept, *later[1], *state, back_stay, pack_stay, summed],
        scratch,
    )
    new_amax = jnp.max(column_max, axis=1).reshape(block_count, 1)
    packed = call(
        packing_kernel,
        shape(row_count, TILE),
        [VMEM] * 3,
        [arrived, pack_go, packed],
    )
    incoming = lax.all_to_all(
        packed.reshape(row_count // 2, 2, TILE),
        "fsdp",
        split_axis=0,
        concat_axis=0,
        axis_index_groups=[list(range(half)), list(range(half, owner_count))],
        tiled=True,
    ).reshape(row_count, TILE)
    new_rollout = call(
        adding_kernel,
        shape(row_count, TILE),
        [VMEM] * 3,
        [incoming, order, rollout],
    )
    return (new_master, new_one, new_two, new_amax, new_rollout)


def solution(mesh):
    return jax.shard_map(
        body,
        mesh=mesh,
        in_specs=(
            P("dp", "fsdp", None),
            P("fsdp", "dp"),
            P("fsdp", "dp"),
            P("fsdp", "dp"),
            P("fsdp", "dp"),
            P("fsdp", "dp"),
            P("fsdp", "dp"),
            P(),
            P(),
        ),
        out_specs=(
            P("fsdp", "dp"),
            P("fsdp", "dp"),
            P("fsdp", "dp"),
            P("fsdp", "dp"),
            P("fsdp", "dp"),
        ),
        check_vma=False,
    )
```

```python
import functools

import jax
import jax.numpy as jnp
from jax import lax
from jax.experimental import pallas as pl
from jax.experimental.pallas import tpu as pltpu
from jax.sharding import PartitionSpec as P

D = 7168
TILE = 128
HALF = TILE // 2

beta_one = 0.9
beta_two = 0.95
bias_one = 1.0 - 0.9**10
bias_two = 1.0 - 0.95**10
step_size = 0.05
weight_decay = 0.1
adam_floor = 1e-08

VMEM = pl.BlockSpec(memory_space=pltpu.VMEM)
SMEM = pl.BlockSpec(memory_space=pltpu.SMEM)
ANY = pl.BlockSpec(memory_space=pl.ANY)
F32 = jnp.float32
BF16 = jnp.bfloat16


def adam_step(master, moment_one, moment_two, gradient):
    new_one = beta_one * moment_one + (1.0 - beta_one) * gradient
    new_two = beta_two * moment_two + (1.0 - beta_two) * gradient * gradient
    update = new_one / bias_one / (jnp.sqrt(new_two / bias_two) + adam_floor)
    new_master = master - step_size * (update + weight_decay * master)
    return (new_master, new_one, new_two)


def call(kernel, outs, ins, args, scratch=(), bytes_accessed=2**20):
    single = not isinstance(outs, (tuple, list))
    return pl.pallas_call(
        kernel,
        out_shape=outs,
        in_specs=ins,
        out_specs=VMEM if single else (VMEM,) * len(outs),
        scratch_shapes=list(scratch),
        compiler_params=pltpu.CompilerParams(vmem_limit_bytes=16 * 2**20),
        cost_estimate=pl.CostEstimate(
            flops=bytes_accessed, bytes_accessed=bytes_accessed, transcendentals=0
        ),
    )(*args)


def exchange(x, axis, distance, count):
    return lax.ppermute(x, axis, [(i, i ^ distance) for i in range(count)])


def ranks(across, axis):
    i = lax.broadcasted_iota(jnp.int32, (TILE, TILE), 1 - axis)
    j = lax.broadcasted_iota(jnp.int32, (TILE, TILE), axis)
    down = jnp.sum(jnp.where(i == j, across, 0), axis=1, keepdims=True)
    mine, other = (across, down) if axis == 0 else (down, across)
    before = (other < mine) | ((other == mine) & (j < i))
    return jnp.sum(before.astype(jnp.int32), axis=axis, keepdims=True)


def owners_of(rank, block, expert_owner, owner_count, block_count):
    per_owner = TILE // owner_count
    expert = (lax.axis_index("fsdp") * block_count + block) * TILE // D
    turned = rank // per_owner + expert_owner[expert]
    owner = jnp.where(turned >= owner_count, turned - owner_count, turned)
    half = owner_count // 2
    top = (owner >= half).astype(jnp.int32)
    inner = owner - top * half
    here = (lax.axis_index("fsdp") >= half).astype(jnp.int32)
    stays = (top == here).astype(jnp.int32)
    pair = rank - rank // per_owner * per_owner
    return inner, pair, stays, here


def picking_kernel(owner_count, across, expert_owner, picks):
    per_owner = TILE // owner_count
    block_count = picks.shape[0] // TILE
    rank = ranks(across[...], 0)
    place = lax.broadcasted_iota(jnp.int32, (HALF, TILE), 0)
    for block in range(block_count):
        inner, pair, stays, _ = owners_of(rank, block, expert_owner, owner_count, block_count)
        slot = inner * per_owner + pair + stays * HALF
        for chunk in range(2):
            at = (chunk * block_count + block) * HALF
            picks[pl.ds(at, HALF)] = (place + chunk * HALF == slot).astype(F32).astype(BF16)


def placing_kernel(
    owner_count,
    across,
    expert_owner,
    core,
    back_go,
    back_stay,
    pick_go,
    pack_stay,
    pack_go,
    order,
):
    del core
    per_owner = TILE // owner_count
    row_count = back_go.shape[0]
    block_count = row_count // TILE
    chunk_rows = row_count // 2
    along = ranks(across[...], 0)
    upright = ranks(across[...], 1)
    lanes = lax.broadcasted_iota(jnp.int32, (TILE, chunk_rows), 1)
    sublanes = lax.broadcasted_iota(jnp.int32, (row_count, TILE), 0)
    for block in range(block_count):
        at = pl.ds(block * TILE, TILE)
        inner, pair, stays, _ = owners_of(upright, block, expert_owner, owner_count, block_count)
        slot = block * HALF + inner * per_owner + pair
        back_go[at] = (lanes == jnp.where(stays == 0, slot, -1)).astype(F32).astype(BF16)
        back_stay[at] = (lanes == jnp.where(stays == 1, slot, -1)).astype(F32).astype(BF16)
        inner, pair, stays, here = owners_of(along, block, expert_owner, owner_count, block_count)
        slot = block * HALF + inner * per_owner + pair
        pick_go[:, at] = (
            (sublanes[:chunk_rows] == jnp.where(stays == 0, slot, -1)).astype(F32).astype(BF16)
        )
        sent = ((inner * 2 + here) * block_count + block) * per_owner + pair
        pack_stay[:, at] = (sublanes == jnp.where(stays == 1, sent, -1)).astype(F32).astype(BF16)

    half = owner_count // 2
    there = 1 - (lax.axis_index("fsdp") >= half).astype(jnp.int32)
    row = lax.broadcasted_iota(jnp.int32, (1, chunk_rows), 1)
    block = row // HALF
    inner = (row - block * HALF) // per_owner
    pair = row - row // per_owner * per_owner
    sent = ((inner * 2 + there) * block_count + block) * per_owner + pair
    pack_go[...] = (
        (lax.broadcasted_iota(jnp.int32, (row_count, chunk_rows), 0) == sent).astype(F32).astype(BF16)
    )

    group = block_count * per_owner
    row = lax.broadcasted_iota(jnp.int32, (1, row_count), 1)
    source = row // group
    wanted = ((source & 1) * half + (source >> 1)) * group + (row - source * group)
    order[...] = (
        (lax.broadcasted_iota(jnp.int32, (row_count, row_count), 0) == wanted).astype(F32).astype(BF16)
    )


def keeping_kernel(gradients, out, arrived):
    core = lax.axis_index("dp") & 1
    copies = []
    for q in range(out.shape[0]):
        columns = pl.ds(pl.multiple_of((2 * q + core) * TILE, TILE), TILE)
        copy = pltpu.make_async_copy(gradients.at[0, :, columns], out.at[q], arrived.at[q])
        copy.start()
        copies.append(copy)
    for copy in copies:
        copy.wait()


def first_kernel(sent, chunks, own, core, picks, *rest):
    out = rest[-1]
    place = lax.axis_index("dp")
    count, block_count = out.shape[0], own.shape[1] // TILE
    bit = (place >> 1) & 1
    wanted = (1 - bit) if sent else bit
    for r in range(block_count):
        at = pl.ds(r * TILE, TILE)
        sums = []
        for q in range(count):
            block = (q << 2) | (wanted << 1) | (place & 1)
            columns = pl.ds(pl.multiple_of(block * TILE, TILE), TILE)
            sums.append((own[block >> 1, at].astype(F32) + core[0, at, columns].astype(F32)).astype(BF16))
        joined = jnp.concatenate(sums, axis=1)
        for n, chunk in enumerate(chunks):
            pick = picks[pl.ds((chunk * block_count + r) * HALF, HALF)]
            moved = jnp.dot(pick, joined, preferred_element_type=F32).astype(BF16)
            for q in range(count):
                out[q, pl.ds((n * block_count + r) * HALF, HALF)] = moved[:, q * TILE : (q + 1) * TILE]


def sum_so_far(block, chunk, kept, later):
    rows = later[0].shape[1]
    total = kept[block >> 2, pl.ds(chunk * rows, rows)].astype(F32)
    for step, received in enumerate(later):
        total = total + received[block >> (step + 2)].astype(F32)
    return total


def sending_kernel(bit, chunk, count, kept, *rest):
    later, out = rest[:count], rest[-1]
    place = lax.axis_index("dp")
    low = place & ((1 << bit) - 1)
    other = (1 - ((place >> bit) & 1)) << bit
    for q in range(out.shape[0]):
        block = (q << (bit + 1)) | other | low
        out[q] = sum_so_far(block, chunk, kept, later).astype(BF16)


def in_two(total, parts):
    high = total.astype(BF16)
    parts[:, :TILE] = high
    parts[:, TILE:] = (total - high.astype(F32)).astype(BF16)


def preparing_kernel(master, one, two, synced, pick, received, based, ones, twos, parts):
    del received
    based_all = master[...] * (1.0 - step_size * weight_decay) - synced[...].astype(F32)
    for value, out in (
        (based_all, based),
        (beta_one * one[...], ones),
        (beta_two * two[...], twos),
    ):
        in_two(value, parts)
        pieces = jnp.dot(pick[...], parts[...], preferred_element_type=F32)
        out[...] = pieces[:, :TILE] + pieces[:, TILE:]


def going_kernel(steps, replica_count, kept, *rest):
    later = rest[:steps]
    based, ones, twos, record, outgoing = rest[steps:]
    gradient = sum_so_far(lax.axis_index("dp"), 0, kept, later) / replica_count
    new_one = ones[...] + (1.0 - beta_one) * gradient
    new_two = twos[...] + (1.0 - beta_two) * gradient * gradient
    update = new_one / bias_one / (jnp.sqrt(new_two / bias_two) + adam_floor)
    delta = based[...] - step_size * update
    for tile in range(delta.shape[0] // HALF):
        limit = record[0, tile]
        rows = delta[tile * HALF : (tile + 1) * HALF]
        outgoing[pl.ds(tile * HALF, HALF)] = jnp.clip(rows, -limit, limit).astype(BF16)


def staying_kernel(steps, replica_count, kept, *rest):
    go, stay, rest = rest[:steps], rest[steps : 2 * steps], rest[2 * steps :]
    master, one, two, synced, record, back_go, back_stay, pack = rest[:8]
    new_master, new_one, new_two, column_max, packed, parts_go, parts_stay, clipped = rest[8:]
    place = lax.axis_index("dp")
    in_two(sum_so_far(place, 0, kept, go), parts_go)
    in_two(sum_so_far(place, 1, kept, stay), parts_stay)
    for tile in range(master.shape[0] // TILE):
        at = pl.ds(tile * TILE, TILE)
        pieces = jnp.dot(back_go[at], parts_go[...], preferred_element_type=F32)
        pieces = pieces + jnp.dot(back_stay[at], parts_stay[...], preferred_element_type=F32)
        total = pieces[:, :TILE] + pieces[:, TILE:]
        a, b, c = adam_step(master[at], one[at], two[at], total / replica_count)
        new_master[at] = a
        new_one[at] = b
        new_two[at] = c
        delta = a - synced[at].astype(F32)
        column_max[pl.ds(tile, 1)] = jnp.max(jnp.abs(delta), axis=0, keepdims=True)
        limit = record[0, tile]
        clipped[at] = jnp.clip(delta, -limit, limit).astype(BF16)
    packed[...] = jnp.dot(pack[...], clipped[...], preferred_element_type=F32).astype(BF16)


def packing_kernel(arrived, pack, staying, out):
    moved = jnp.dot(pack[...], arrived[...], preferred_element_type=F32)
    out[...] = (moved + staying[...].astype(F32)).astype(BF16)


def adding_kernel(incoming, order, rollout, out):
    moved = jnp.dot(order[...], incoming[...], preferred_element_type=F32)
    out[...] = (rollout[...].astype(F32) + moved).astype(BF16)


def body(
    gradients, master, moment_one, moment_two, synced, rollout, amax_record, row_table, expert_owner
):
    owner_count = lax.axis_size("fsdp")
    replica_count = lax.axis_size("dp")
    row_count, column_count = master.shape
    block_count = row_count // TILE
    rows = row_count // 2
    half = owner_count // 2

    def shape(*dims, dtype=BF16):
        return jax.ShapeDtypeStruct(dims, dtype)

    core = exchange(gradients, "dp", 1, replica_count)
    own = call(
        keeping_kernel,
        shape(replica_count // 2, row_count, TILE),
        [ANY],
        [gradients],
        [pltpu.SemaphoreType.DMA((replica_count // 2,))],
    )
    table = [row_table.reshape(1, TILE), expert_owner]
    table_specs = [VMEM, SMEM]
    picks = call(
        functools.partial(picking_kernel, owner_count), shape(row_count, TILE), table_specs, table
    )

    later = [[], []]
    steps = replica_count.bit_length() - 2
    sent = shape(replica_count // 4, rows, TILE)
    summands = [own, core, picks]
    first = call(functools.partial(first_kernel, True, (0,)), sent, [VMEM] * 3, summands)
    later[0].append(exchange(first, "dp", 2, replica_count))
    kept = call(
        functools.partial(first_kernel, False, (0, 1)),
        shape(replica_count // 4, row_count, TILE),
        [VMEM] * 3,
        summands,
    )
    back_go, back_stay, pick_go, pack_stay, pack_go, order = call(
        functools.partial(placing_kernel, owner_count),
        (
            shape(row_count, rows),
            shape(row_count, rows),
            shape(rows, row_count),
            shape(row_count, row_count),
            shape(row_count, rows),
            shape(row_count, row_count),
        ),
        [*table_specs, ANY],
        [*table, core],
    )
    second = call(
        functools.partial(first_kernel, True, (1,)),
        sent,
        [VMEM] * 3 + [ANY] * 2,
        [*summands, kept, pick_go],
    )
    later[1].append(exchange(second, "dp", 2, replica_count))
    state = [master, moment_one, moment_two, synced]
    record = amax_record.reshape(1, block_count)
    going = shape(rows, TILE, dtype=F32)
    for bit in range(2, steps + 1):
        for chunk in range(2):
            ahead = []
            if bit == 2 and chunk == 1:
                prepared = call(
                    preparing_kernel,
                    (going, going, going),
                    [VMEM] * 5 + [ANY],
                    [*state, pick_go, later[0][0]],
                    [pltpu.VMEM((row_count, 2 * TILE), BF16)],
                )
                ahead = [prepared[0]]
            count = len(later[chunk])
            out = call(
                functools.partial(sending_kernel, bit, chunk, count),
                shape(replica_count >> (bit + 1), rows, TILE),
                [VMEM] * (1 + count) + [ANY] * len(ahead),
                [kept, *later[chunk], *ahead],
            )
            later[chunk].append(exchange(out, "dp", 1 << bit, replica_count))

    outgoing = call(
        functools.partial(going_kernel, steps, replica_count),
        shape(rows, TILE),
        [VMEM] * (1 + steps + 3) + [SMEM],
        [kept, *later[0], *prepared, record],
    )
    arrived = exchange(outgoing, "fsdp", half, owner_count)
    full = shape(row_count, TILE, dtype=F32)
    new_master, new_one, new_two, column_max, packed = call(
        functools.partial(staying_kernel, steps, replica_count),
        (full, full, full, shape(block_count, TILE, dtype=F32), shape(row_count, TILE)),
        [VMEM] * (1 + 2 * steps + 4) + [SMEM] + [VMEM] * 3,
        [kept, *later[0], *later[1], *state, record, back_go, back_stay, pack_stay],
        [
            pltpu.VMEM((rows, 2 * TILE), BF16),
            pltpu.VMEM((rows, 2 * TILE), BF16),
            pltpu.VMEM((row_count, TILE), BF16),
        ],
    )
    new_amax = jnp.max(column_max, axis=1).reshape(block_count, 1)
    packed = call(
        packing_kernel,
        shape(row_count, TILE),
        [VMEM] * 3,
        [arrived, pack_go, packed],
    )
    incoming = lax.all_to_all(
        packed.reshape(row_count // 2, 2, TILE),
        "fsdp",
        split_axis=0,
        concat_axis=0,
        axis_index_groups=[list(range(half)), list(range(half, owner_count))],
        tiled=True,
    ).reshape(row_count, TILE)
    new_rollout = call(
        adding_kernel,
        shape(row_count, TILE),
        [VMEM] * 3,
        [incoming, order, rollout],
    )
    return (new_master, new_one, new_two, new_amax, new_rollout)


def solution(mesh):
    return jax.shard_map(
        body,
        mesh=mesh,
        in_specs=(
            P("dp", "fsdp", None),
            P("fsdp", "dp"),
            P("fsdp", "dp"),
            P("fsdp", "dp"),
            P("fsdp", "dp"),
            P("fsdp", "dp"),
            P("fsdp", "dp"),
            P(),
            P(),
        ),
        out_specs=(
            P("fsdp", "dp"),
            P("fsdp", "dp"),
            P("fsdp", "dp"),
            P("fsdp", "dp"),
            P("fsdp", "dp"),
        ),
        check_vma=False,
    )
```

```python
import functools

import jax
import jax.numpy as jnp
from jax import lax
from jax.experimental import pallas as pl
from jax.experimental.pallas import tpu as pltpu
from jax.sharding import PartitionSpec as P

D = 7168
TILE = 128
HALF = TILE // 2

beta_one = 0.9
beta_two = 0.95
bias_one = 1.0 - 0.9**10
bias_two = 1.0 - 0.95**10
step_size = 0.05
weight_decay = 0.1
adam_floor = 1e-08

VMEM = pl.BlockSpec(memory_space=pltpu.VMEM)
SMEM = pl.BlockSpec(memory_space=pltpu.SMEM)
ANY = pl.BlockSpec(memory_space=pl.ANY)
F32 = jnp.float32
BF16 = jnp.bfloat16


def adam_step(master, moment_one, moment_two, gradient):
    new_one = beta_one * moment_one + (1.0 - beta_one) * gradient
    new_two = beta_two * moment_two + (1.0 - beta_two) * gradient * gradient
    update = new_one / bias_one / (jnp.sqrt(new_two / bias_two) + adam_floor)
    new_master = master - step_size * (update + weight_decay * master)
    return (new_master, new_one, new_two)


def call(kernel, outs, ins, args, scratch=(), bytes_accessed=2**20):
    single = not isinstance(outs, (tuple, list))
    return pl.pallas_call(
        kernel,
        out_shape=outs,
        in_specs=ins,
        out_specs=VMEM if single else (VMEM,) * len(outs),
        scratch_shapes=list(scratch),
        compiler_params=pltpu.CompilerParams(vmem_limit_bytes=16 * 2**20),
        cost_estimate=pl.CostEstimate(
            flops=bytes_accessed, bytes_accessed=bytes_accessed, transcendentals=0
        ),
    )(*args)


def exchange(x, axis, distance, count):
    return lax.ppermute(x, axis, [(i, i ^ distance) for i in range(count)])


def ranks(across, axis):
    i = lax.broadcasted_iota(jnp.int32, (TILE, TILE), 1 - axis)
    j = lax.broadcasted_iota(jnp.int32, (TILE, TILE), axis)
    down = jnp.sum(jnp.where(i == j, across, 0), axis=1, keepdims=True)
    mine, other = (across, down) if axis == 0 else (down, across)
    before = (other < mine) | ((other == mine) & (j < i))
    return jnp.sum(before.astype(jnp.int32), axis=axis, keepdims=True)


def owners_of(rank, block, expert_owner, owner_count, block_count):
    per_owner = TILE // owner_count
    expert = (lax.axis_index("fsdp") * block_count + block) * TILE // D
    turned = rank // per_owner + expert_owner[expert]
    owner = jnp.where(turned >= owner_count, turned - owner_count, turned)
    half = owner_count // 2
    top = (owner >= half).astype(jnp.int32)
    inner = owner - top * half
    here = (lax.axis_index("fsdp") >= half).astype(jnp.int32)
    stays = (top == here).astype(jnp.int32)
    pair = rank - rank // per_owner * per_owner
    return inner, pair, stays, here


def picking_kernel(owner_count, across, expert_owner, picks):
    per_owner = TILE // owner_count
    block_count = picks.shape[0] // TILE
    rank = ranks(across[...], 0)
    place = lax.broadcasted_iota(jnp.int32, (HALF, TILE), 0)
    for block in range(block_count):
        inner, pair, stays, _ = owners_of(rank, block, expert_owner, owner_count, block_count)
        slot = inner * per_owner + pair + stays * HALF
        for chunk in range(2):
            at = (chunk * block_count + block) * HALF
            picks[pl.ds(at, HALF)] = (place + chunk * HALF == slot).astype(F32).astype(BF16)


def placing_kernel(
    owner_count,
    across,
    expert_owner,
    core,
    back_go,
    back_stay,
    pick_go,
    pack_stay,
    pack_go,
    order,
):
    del core
    per_owner = TILE // owner_count
    row_count = back_go.shape[0]
    block_count = row_count // TILE
    chunk_rows = row_count // 2
    along = ranks(across[...], 0)
    upright = ranks(across[...], 1)
    lanes = lax.broadcasted_iota(jnp.int32, (TILE, chunk_rows), 1)
    sublanes = lax.broadcasted_iota(jnp.int32, (row_count, TILE), 0)
    for block in range(block_count):
        at = pl.ds(block * TILE, TILE)
        inner, pair, stays, _ = owners_of(upright, block, expert_owner, owner_count, block_count)
        slot = block * HALF + inner * per_owner + pair
        back_go[at] = (lanes == jnp.where(stays == 0, slot, -1)).astype(F32).astype(BF16)
        back_stay[at] = (lanes == jnp.where(stays == 1, slot, -1)).astype(F32).astype(BF16)
        inner, pair, stays, here = owners_of(along, block, expert_owner, owner_count, block_count)
        slot = block * HALF + inner * per_owner + pair
        pick_go[:, at] = (
            (sublanes[:chunk_rows] == jnp.where(stays == 0, slot, -1)).astype(F32).astype(BF16)
        )
        sent = ((inner * 2 + here) * block_count + block) * per_owner + pair
        pack_stay[:, at] = (sublanes == jnp.where(stays == 1, sent, -1)).astype(F32).astype(BF16)

    half = owner_count // 2
    there = 1 - (lax.axis_index("fsdp") >= half).astype(jnp.int32)
    row = lax.broadcasted_iota(jnp.int32, (1, chunk_rows), 1)
    block = row // HALF
    inner = (row - block * HALF) // per_owner
    pair = row - row // per_owner * per_owner
    sent = ((inner * 2 + there) * block_count + block) * per_owner + pair
    pack_go[...] = (
        (lax.broadcasted_iota(jnp.int32, (row_count, chunk_rows), 0) == sent).astype(F32).astype(BF16)
    )

    group = block_count * per_owner
    row = lax.broadcasted_iota(jnp.int32, (1, row_count), 1)
    source = row // group
    wanted = ((source & 1) * half + (source >> 1)) * group + (row - source * group)
    order[...] = (
        (lax.broadcasted_iota(jnp.int32, (row_count, row_count), 0) == wanted).astype(F32).astype(BF16)
    )


def keeping_kernel(gradients, out, arrived):
    core = lax.axis_index("dp") & 1
    copies = []
    for q in range(out.shape[0]):
        columns = pl.ds(pl.multiple_of((2 * q + core) * TILE, TILE), TILE)
        copy = pltpu.make_async_copy(gradients.at[0, :, columns], out.at[q], arrived.at[q])
        copy.start()
        copies.append(copy)
    for copy in copies:
        copy.wait()


def first_kernel(sent, chunks, own, core, picks, *rest):
    out = rest[-1]
    place = lax.axis_index("dp")
    count, block_count = out.shape[0], own.shape[1] // TILE
    bit = (place >> 1) & 1
    wanted = (1 - bit) if sent else bit
    for r in range(block_count):
        at = pl.ds(r * TILE, TILE)
        sums = []
        for q in range(count):
            block = (q << 2) | (wanted << 1) | (place & 1)
            columns = pl.ds(pl.multiple_of(block * TILE, TILE), TILE)
            sums.append((own[block >> 1, at].astype(F32) + core[0, at, columns].astype(F32)).astype(BF16))
        joined = jnp.concatenate(sums, axis=1)
        for n, chunk in enumerate(chunks):
            pick = picks[pl.ds((chunk * block_count + r) * HALF, HALF)]
            moved = jnp.dot(pick, joined, preferred_element_type=F32).astype(BF16)
            for q in range(count):
                out[q, pl.ds((n * block_count + r) * HALF, HALF)] = moved[:, q * TILE : (q + 1) * TILE]


def sum_so_far(block, chunk, kept, later):
    rows = later[0].shape[1]
    total = kept[block >> 2, pl.ds(chunk * rows, rows)].astype(F32)
    for step, received in enumerate(later):
        total = total + received[block >> (step + 2)].astype(F32)
    return total


def sending_kernel(bit, chunk, count, kept, *rest):
    later, out = rest[:count], rest[-1]
    place = lax.axis_index("dp")
    low = place & ((1 << bit) - 1)
    other = (1 - ((place >> bit) & 1)) << bit
    for q in range(out.shape[0]):
        block = (q << (bit + 1)) | other | low
        out[q] = sum_so_far(block, chunk, kept, later).astype(BF16)


def in_two(total, parts):
    high = total.astype(BF16)
    parts[:, :TILE] = high
    parts[:, TILE:] = (total - high.astype(F32)).astype(BF16)


def preparing_kernel(master, one, two, synced, pick, received, based, ones, twos, parts):
    del received
    based_all = master[...] * (1.0 - step_size * weight_decay) - synced[...].astype(F32)
    for value, out in (
        (based_all, based),
        (beta_one * one[...], ones),
        (beta_two * two[...], twos),
    ):
        in_two(value, parts)
        pieces = jnp.dot(pick[...], parts[...], preferred_element_type=F32)
        out[...] = pieces[:, :TILE] + pieces[:, TILE:]


def going_kernel(steps, replica_count, kept, *rest):
    later = rest[:steps]
    based, ones, twos, record, outgoing = rest[steps:]
    gradient = sum_so_far(lax.axis_index("dp"), 0, kept, later) / replica_count
    new_one = ones[...] + (1.0 - beta_one) * gradient
    new_two = twos[...] + (1.0 - beta_two) * gradient * gradient
    update = new_one / bias_one / (jnp.sqrt(new_two / bias_two) + adam_floor)
    delta = based[...] - step_size * update
    for tile in range(delta.shape[0] // HALF):
        limit = record[0, tile]
        rows = delta[tile * HALF : (tile + 1) * HALF]
        outgoing[pl.ds(tile * HALF, HALF)] = jnp.clip(rows, -limit, limit).astype(BF16)


def staying_kernel(steps, replica_count, kept, *rest):
    go, stay, rest = rest[:steps], rest[steps : 2 * steps], rest[2 * steps :]
    master, one, two, synced, record, back_go, back_stay, pack = rest[:8]
    new_master, new_one, new_two, column_max, packed, parts_go, parts_stay, clipped = rest[8:]
    place = lax.axis_index("dp")
    in_two(sum_so_far(place, 0, kept, go), parts_go)
    in_two(sum_so_far(place, 1, kept, stay), parts_stay)
    for tile in range(master.shape[0] // TILE):
        at = pl.ds(tile * TILE, TILE)
        pieces = jnp.dot(back_go[at], parts_go[...], preferred_element_type=F32)
        pieces = pieces + jnp.dot(back_stay[at], parts_stay[...], preferred_element_type=F32)
        total = pieces[:, :TILE] + pieces[:, TILE:]
        a, b, c = adam_step(master[at], one[at], two[at], total / replica_count)
        new_master[at] = a
        new_one[at] = b
        new_two[at] = c
        delta = a - synced[at].astype(F32)
        column_max[pl.ds(tile, 1)] = jnp.max(jnp.abs(delta), axis=0, keepdims=True)
        limit = record[0, tile]
        clipped[at] = jnp.clip(delta, -limit, limit).astype(BF16)
    packed[...] = jnp.dot(pack[...], clipped[...], preferred_element_type=F32).astype(BF16)


def packing_kernel(arrived, pack, staying, out):
    moved = jnp.dot(pack[...], arrived[...], preferred_element_type=F32)
    out[...] = (moved + staying[...].astype(F32)).astype(BF16)


def adding_kernel(incoming, order, rollout, out):
    moved = jnp.dot(order[...], incoming[...], preferred_element_type=F32)
    out[...] = (rollout[...].astype(F32) + moved).astype(BF16)


def body(
    gradients, master, moment_one, moment_two, synced, rollout, amax_record, row_table, expert_owner
):
    owner_count = lax.axis_size("fsdp")
    replica_count = lax.axis_size("dp")
    row_count, column_count = master.shape
    block_count = row_count // TILE
    rows = row_count // 2
    half = owner_count // 2

    def shape(*dims, dtype=BF16):
        return jax.ShapeDtypeStruct(dims, dtype)

    core = exchange(gradients, "dp", 1, replica_count)
    own = call(
        keeping_kernel,
        shape(replica_count // 2, row_count, TILE),
        [ANY],
        [gradients],
        [pltpu.SemaphoreType.DMA((replica_count // 2,))],
    )
    table = [row_table.reshape(1, TILE), expert_owner]
    table_specs = [VMEM, SMEM]
    picks = call(
        functools.partial(picking_kernel, owner_count), shape(row_count, TILE), table_specs, table
    )

    later = [[], []]
    steps = replica_count.bit_length() - 2
    sent = shape(replica_count // 4, rows, TILE)
    summands = [own, core, picks]
    first = call(functools.partial(first_kernel, True, (0,)), sent, [VMEM] * 3, summands)
    later[0].append(exchange(first, "dp", 2, replica_count))
    kept = call(
        functools.partial(first_kernel, False, (0, 1)),
        shape(replica_count // 4, row_count, TILE),
        [VMEM] * 3,
        summands,
    )
    back_go, back_stay, pick_go, pack_stay, pack_go, order = call(
        functools.partial(placing_kernel, owner_count),
        (
            shape(row_count, rows),
            shape(row_count, rows),
            shape(rows, row_count),
            shape(row_count, row_count),
            shape(row_count, rows),
            shape(row_count, row_count),
        ),
        [*table_specs, ANY],
        [*table, core],
    )
    second = call(functools.partial(first_kernel, True, (1,)), sent, [VMEM] * 3, summands)
    later[1].append(exchange(second, "dp", 2, replica_count))
    state = [master, moment_one, moment_two, synced]
    record = amax_record.reshape(1, block_count)
    going = shape(rows, TILE, dtype=F32)
    for bit in range(2, steps + 1):
        for chunk in range(2):
            ahead = [pick_go] if bit == 2 else []
            if bit == 2 and chunk == 1:
                prepared = call(
                    preparing_kernel,
                    (going, going, going),
                    [VMEM] * 5 + [ANY],
                    [*state, pick_go, later[0][0]],
                    [pltpu.VMEM((row_count, 2 * TILE), BF16)],
                )
                ahead = [prepared[0]]
            count = len(later[chunk])
            out = call(
                functools.partial(sending_kernel, bit, chunk, count),
                shape(replica_count >> (bit + 1), rows, TILE),
                [VMEM] * (1 + count) + [ANY] * len(ahead),
                [kept, *later[chunk], *ahead],
            )
            later[chunk].append(exchange(out, "dp", 1 << bit, replica_count))

    outgoing = call(
        functools.partial(going_kernel, steps, replica_count),
        shape(rows, TILE),
        [VMEM] * (1 + steps + 3) + [SMEM],
        [kept, *later[0], *prepared, record],
    )
    arrived = exchange(outgoing, "fsdp", half, owner_count)
    full = shape(row_count, TILE, dtype=F32)
    new_master, new_one, new_two, column_max, packed = call(
        functools.partial(staying_kernel, steps, replica_count),
        (full, full, full, shape(block_count, TILE, dtype=F32), shape(row_count, TILE)),
        [VMEM] * (1 + 2 * steps + 4) + [SMEM] + [VMEM] * 3,
        [kept, *later[0], *later[1], *state, record, back_go, back_stay, pack_stay],
        [
            pltpu.VMEM((rows, 2 * TILE), BF16),
            pltpu.VMEM((rows, 2 * TILE), BF16),
            pltpu.VMEM((row_count, TILE), BF16),
        ],
    )
    new_amax = jnp.max(column_max, axis=1).reshape(block_count, 1)
    packed = call(
        packing_kernel,
        shape(row_count, TILE),
        [VMEM] * 3,
        [arrived, pack_go, packed],
    )
    incoming = lax.all_to_all(
        packed.reshape(row_count // 2, 2, TILE),
        "fsdp",
        split_axis=0,
        concat_axis=0,
        axis_index_groups=[list(range(half)), list(range(half, owner_count))],
        tiled=True,
    ).reshape(row_count, TILE)
    new_rollout = call(
        adding_kernel,
        shape(row_count, TILE),
        [VMEM] * 3,
        [incoming, order, rollout],
    )
    return (new_master, new_one, new_two, new_amax, new_rollout)


def solution(mesh):
    return jax.shard_map(
        body,
        mesh=mesh,
        in_specs=(
            P("dp", "fsdp", None),
            P("fsdp", "dp"),
            P("fsdp", "dp"),
            P("fsdp", "dp"),
            P("fsdp", "dp"),
            P("fsdp", "dp"),
            P("fsdp", "dp"),
            P(),
            P(),
        ),
        out_specs=(
            P("fsdp", "dp"),
            P("fsdp", "dp"),
            P("fsdp", "dp"),
            P("fsdp", "dp"),
            P("fsdp", "dp"),
        ),
        check_vma=False,
    )
```
